256 devices in a mesh: wide: 16 (over z, x_hi), narrow: 16 (over x_lo, y, core).
Axes of the slice: x: 4 (x_hi: 2, x_lo: 2; x = x_hi * 2 + x_lo), y: 4, z: 8, core: 2. Of those that a mesh axis runs over, the one named last changes fastest.
Arguments:
- activations: bfloat16 [1536, 4096], P('narrow', 'wide'), may hold values from -6 to 6
- grad_outputs: bfloat16 [1536, 14336], P('wide', 'narrow'), may hold values from -0.75 to 0.75
- act_basis: bfloat16 [4096, 4096], P('wide', 'narrow'), may hold values from -0.09375 to 0.09375
- grad_basis: bfloat16 [14336, 14336], P('narrow', 'wide'), may hold values from -0.046875 to 0.046875
Outputs:
- eigenvalues: float32 [4096, 14336], P('narrow', 'wide')
The draws below stay inside these ranges and needn't reach their ends.
All inputs are finite; a program needn't handle non-finite values.
Results may differ from the reference program's by a relative error of at most 0.0034.
Values may be sent and summed in bfloat16 or wider, within the bound.
No kernel may reach another device: no remote copies, remote signals or barrier semaphores. Data moves between devices by JAX's collectives and lax.ppermute only.
A program may use at most 64 MiB of HBM per device.

```python
import jax
import jax.numpy as jnp
from jax import lax

DIN = 4096
DOUT = 14336
SEQS = 4
SEQ_LEN = 384
TOKENS = 1536
N_WIDE = 16
N_NARROW = 16


def levels(rng, shape, cuts, low, largest):
    def one(position, blocks):
        steps = jax.random.uniform(jax.random.fold_in(jax.random.fold_in(rng, 6), position), (blocks,), jnp.float32, low / len(cuts), largest / len(cuts))
        return jnp.repeat(jnp.exp(steps), shape[position] // blocks).reshape((-1,) + (1,) * (len(shape) - position - 1))

    gain = one(*cuts[0])
    for cut in cuts[1:]:
        gain = gain * one(*cut)
    return gain


def normal_values(own_key, dims, scale, reach, shards=(), dtype=jnp.bfloat16):
    result = scale * jax.random.normal(own_key, dims, jnp.float32)
    if shards:
        result = result * levels(own_key, dims, shards, -0.22, 0.18)
    return jnp.clip(result, -reach, reach).astype(dtype)


def setup_inputs(seed: int = 0) -> dict:
    keys = jax.random.split(jax.random.key(seed), 5)
    activations = normal_values(keys[0], (TOKENS, DIN), 1.0, 6.0, ((0, 16), (1, 16)))
    grad_outputs = normal_values(keys[1], (TOKENS, DOUT), (SEQ_LEN ** -0.5), 0.75, ((0, 16), (1, 16)))
    act_basis = normal_values(keys[2], (DIN, DIN), DIN ** -0.5, 0.09375, ((0, 16), (1, 16)))
    grad_basis = normal_values(keys[3], (DOUT, DOUT), DOUT ** -0.5, 0.046875, ((0, 16), (1, 16)))
    return dict(activations=activations, grad_outputs=grad_outputs, act_basis=act_basis, grad_basis=grad_basis)


def rotate_blocks(inputs, basis, blocks):
    width = inputs.shape[1] // blocks
    total = jnp.zeros((inputs.shape[0], basis.shape[1]), jnp.float32)
    for index in range(blocks):
        term = jnp.dot(inputs[:, index * width:(index + 1) * width], basis[index * width:(index + 1) * width, :], preferred_element_type=jnp.float32)
        total = total + term
    return total.astype(jnp.bfloat16)


def reference(activations, grad_outputs, act_basis, grad_basis):
    act_rot = rotate_blocks(activations, act_basis, N_WIDE)
    grad_rot = rotate_blocks(grad_outputs, grad_basis, N_NARROW)
    act_seqs = act_rot.reshape(SEQS, SEQ_LEN, DIN)
    grad_seqs = grad_rot.reshape(SEQS, SEQ_LEN, DOUT)

    def accumulate(running, members):
        act_one, grad_one = members
        coeffs = jnp.dot(act_one.T, grad_one, preferred_element_type=jnp.float32)
        return running + coeffs * coeffs, None

    initial = jnp.zeros((DIN, DOUT), jnp.float32)
    summed, unused = lax.scan(accumulate, initial, (act_seqs, grad_seqs))
    return summed / SEQS
```

```python
import jax
import jax.numpy as jnp
from jax import lax
from jax.experimental import pallas as pl
from jax.experimental.pallas import tpu as pltpu
from jax.sharding import Mesh, PartitionSpec as P

SEQS = 4
NZ = 8
CHIPS = ("xl", "y")


def shift(x, axis, by, size):
    return lax.ppermute(x, axis, [(i, (i + by) % size) for i in range(size)])


def swap(x, axis):
    return lax.ppermute(x, axis, [(0, 1), (1, 0)])


def dot(x, y):
    return jnp.dot(x, y, preferred_element_type=jnp.float32)


def spread(x, axis, size):
    copies = jnp.broadcast_to(x[None], (size,) + x.shape).reshape((size * x.shape[0],) + x.shape[1:])
    return lax.all_to_all(copies, axis, 0, 0, tiled=True)


def ring(block, half):
    out = [None] * NZ
    out[0] = up = down = block
    for step in range(1, NZ // 2):
        up = shift(up, "z", 1, NZ)
        down = shift(down, "z", -1, NZ)
        out[NZ - step], out[step] = up, down
    last = (shift(up[:, :half], "z", 1, NZ), shift(down[:, half:], "z", -1, NZ))
    out[NZ // 2] = jnp.concatenate(last, axis=1)
    return out


def coeffs_kernel(where, act, mine, other, out):
    z, d = where[0], where[1]
    total = None
    for seq in range(SEQS):
        left, right = [], []
        for block in (2 * seq, 2 * seq + 1):
            rel = lax.rem(block - z + NZ, NZ)
            left += [act[rel, d, d], act[rel, d, 1 - d], act[rel, 1 - d, d], act[rel, 1 - d, 1 - d]]
            right += [mine[rel], other[rel]]
        coeffs = lax.dot_general(
            jnp.concatenate(left, axis=0),
            jnp.concatenate(right, axis=0),
            (((0,), (0,)), ((), ())),
            preferred_element_type=jnp.float32,
        )
        square = coeffs * coeffs
        total = square if total is None else total + square
    out[...] = total * (1.0 / SEQS)


def per_device(activations, grad_outputs, act_basis, grad_basis):
    z, xh, c = lax.axis_index("z"), lax.axis_index("xh"), lax.axis_index("c")
    rows, half = grad_outputs.shape[0], grad_outputs.shape[0] // 2

    basis = jnp.concatenate([grad_basis, swap(grad_basis, "c")], axis=0)
    both = jnp.concatenate([grad_outputs, swap(grad_outputs, "c")], axis=1)
    block = lax.dynamic_slice(both, (c * half, 0), (half, both.shape[1]))
    mine = ring(block, grad_outputs.shape[1])
    theirs = ring(swap(block, "xh"), grad_outputs.shape[1])

    act_basis2 = jnp.concatenate([act_basis, swap(act_basis, "xh")], axis=0)
    act_both = jnp.concatenate([activations, swap(activations, "xh")], axis=1)
    act_block = lax.dynamic_slice(act_both, (xh * half, 0), (half, act_both.shape[1]))
    act_own = spread(act_block, CHIPS, 8)
    act_oth = swap(act_own, "c")
    act_rows = jnp.stack([act_own.reshape(8, half, -1), act_oth.reshape(8, half, -1)], axis=1)
    act_terms = dot(act_rows.reshape(8 * rows, -1), act_basis2)
    act_sum = lax.psum_scatter(act_terms, "z", scatter_dimension=0, tiled=True).astype(jnp.bfloat16)
    act_pair = jnp.concatenate([act_sum, swap(act_sum, "xh")], axis=0)
    act_all = jnp.stack(ring(act_pair, 128)).reshape(NZ, 2, 2, half, -1)

    terms = [None] * NZ
    for first, second in ((7, 1), (6, 2), (5, 3), (0, 4)):
        x = jnp.concatenate([mine[first], theirs[first], mine[second], theirs[second]], axis=0)
        term = dot(x, basis).astype(jnp.bfloat16)
        terms[first], terms[second] = term[:rows], term[rows:]
    parts = lax.all_to_all(jnp.concatenate(terms, axis=0), CHIPS, 0, 0, tiled=True)
    grad_sum = jnp.sum(parts.reshape(8, rows, -1).astype(jnp.float32), axis=0).astype(jnp.bfloat16)
    grad_own = spread(grad_sum, CHIPS, 8)
    grad_oth = swap(grad_own, "c")

    where = jnp.stack([z, jnp.bitwise_xor(xh, c)]).astype(jnp.int32)
    width = grad_outputs.shape[1]
    return pl.pallas_call(
        coeffs_kernel,
        out_shape=jax.ShapeDtypeStruct((act_basis.shape[1], width), jnp.float32),
        in_specs=[pl.BlockSpec(memory_space=pltpu.SMEM)] + [pl.BlockSpec(memory_space=pltpu.VMEM)] * 3,
        out_specs=pl.BlockSpec(memory_space=pltpu.VMEM),
        compiler_params=pltpu.CompilerParams(vmem_limit_bytes=48 * 1024 * 1024),
        cost_estimate=pl.CostEstimate(flops=703 * 10**6, bytes_accessed=5 * 10**6, transcendentals=0),
    )(where, act_all, grad_own.reshape(NZ, rows, width), grad_oth.reshape(NZ, rows, width))


def solution(mesh):
    fine = Mesh(mesh.devices.reshape(8, 2, 2, 4, 2), ("z", "xh", "xl", "y", "c"))
    wide, narrow = ("z", "xh"), ("xl", "y", "c")
    return jax.shard_map(
        per_device,
        mesh=fine,
        in_specs=(P(narrow, wide), P(wide, narrow), P(wide, narrow), P(narrow, wide)),
        out_specs=P(narrow, wide),
        check_vma=False,
    )
```

```python
import jax
import jax.numpy as jnp
from jax import lax
from jax.experimental import pallas as pl
from jax.experimental.pallas import tpu as pltpu
from jax.sharding import Mesh, PartitionSpec as P

SEQS = 4
NZ = 8
CHIPS, NARROW, WIDE = ("xl", "y"), ("xl", "y", "c"), ("z", "xh")


def shift(x, axis, by, size):
    return lax.ppermute(x, axis, [(i, (i + by) % size) for i in range(size)])


def swap(x, axis):
    return lax.ppermute(x, axis, [(0, 1), (1, 0)])


def dot(x, y):
    return jnp.dot(x, y, preferred_element_type=jnp.float32)


VMEM = pl.BlockSpec(memory_space=pltpu.VMEM)
ANY = pl.BlockSpec(memory_space=pl.ANY)
SMEM = pl.BlockSpec(memory_space=pltpu.SMEM)


def call(body, out, ins, specs, after=(), flops=10**6, moved=10**6, **more):
    def kernel(*refs):
        body(*refs[: len(ins)], *refs[len(ins) + len(after) :])

    return pl.pallas_call(
        kernel,
        out_shape=out,
        in_specs=list(specs) + [ANY] * len(after),
        compiler_params=pltpu.CompilerParams(vmem_limit_bytes=16 * 1024 * 1024),
        cost_estimate=pl.CostEstimate(flops=flops, bytes_accessed=moved, transcendentals=0),
        **more,
    )(*ins, *after)


def gate(live, after=()):
    live = list(live)
    return call(
        lambda *refs: None,
        [jax.ShapeDtypeStruct(x.shape, x.dtype) for x in live],
        live,
        [VMEM] * len(live),
        after,
        out_specs=[VMEM] * len(live),
        input_output_aliases={k: k for k in range(len(live))},
    )


def hop(up, down):
    return shift(up, "z", 1, NZ), shift(down, "z", -1, NZ)


def lap(x):
    steps = [(z, c, (z + 1 - 2 * c) % NZ) for z in range(NZ) for c in (0, 1)]
    return lax.ppermute(x, ("z", "c"), [(2 * z + c, 2 * to + c) for z, c, to in steps])


def pick(where, pairs, after=()):
    def body(where, *refs):
        ins, outs = refs[: 2 * len(pairs)], refs[2 * len(pairs) :]
        for k, out in enumerate(outs):

            @pl.when(where[1] == 0)
            def _():
                out[...] = ins[2 * k][...]

            @pl.when(where[1] != 0)
            def _():
                out[...] = ins[2 * k + 1][...]

    out = [jax.ShapeDtypeStruct(x.shape, x.dtype) for x, _ in pairs]
    ins = [where] + [x for pair in pairs for x in pair]
    return call(body, out, ins, [SMEM] + [VMEM] * (len(ins) - 1), after, out_specs=[VMEM] * len(pairs))


def rotate(blocks, bases, done=(), after=()):
    rows, width = blocks[0][0].shape[0], bases[0].shape[1]
    before = sum(x.shape[0] for x in done)
    parts = [block[0] for block in blocks] + [block[1] for block in blocks]

    def body(*refs):
        refs, (first, second, *done, out) = refs[: len(parts)], refs[len(parts) :]
        left = jnp.concatenate([ref[...] for ref in refs[: len(blocks)]], axis=0)
        right = jnp.concatenate([ref[...] for ref in refs[len(blocks) :]], axis=0)
        out[before:] = (dot(left, first[...]) + dot(right, second[...])).astype(out.dtype)
        for x in done:
            out[:before] = x[...]

    out = jax.ShapeDtypeStruct((before + rows * len(blocks), width), jnp.bfloat16)
    flops = 4 * rows * len(blocks) * width * width
    ins = parts + list(bases) + list(done)
    return call(body, out, ins, [VMEM] * len(ins), after, flops, 6 * 10**6, out_specs=VMEM)


def summed(parts, count, copies, after=()):
    rows, width = parts.shape[0] // count, parts.shape[1]

    def body(x, out):
        total = x[:rows].astype(jnp.float32)
        for k in range(1, count):
            total = total + x[k * rows : (k + 1) * rows].astype(jnp.float32)
        total = total.astype(out.dtype)
        for k in range(copies):
            out[k * rows : (k + 1) * rows] = total

    out = jax.ShapeDtypeStruct((copies * rows, width), jnp.bfloat16)
    return call(body, out, [parts], [VMEM], after, out_specs=VMEM)


def rotate_act(own, other, bases, after=()):
    rows = own.shape[0] // 8
    depth, width = bases[0].shape

    def body(mine, theirs, first, second, out):
        for k, ref in enumerate((mine, theirs)):
            total = dot(ref[:, :depth], first[...]) + dot(ref[:, depth:], second[...])
            for chip in range(8):
                out[chip, k] = total[chip * rows : (chip + 1) * rows]

    out = jax.ShapeDtypeStruct((8, 2, rows, width), jnp.float32)
    return call(body, out, [own, other, *bases], [VMEM] * 4, after, 2 * 10**8, 2 * 10**6, out_specs=VMEM)


def act_halves(where, mine, theirs, after=()):
    half, depth = mine.shape[0] // 2, mine.shape[1]

    def body(where, mine, theirs, out):
        start = pl.multiple_of(where[0] * half, half)
        for k in range(8):
            out[k * half : (k + 1) * half, :depth] = mine[pl.ds(start, half)]
            out[k * half : (k + 1) * half, depth:] = theirs[pl.ds(start, half)]

    out = jax.ShapeDtypeStruct((8 * half, 2 * depth), mine.dtype)
    return call(body, out, [where, mine, theirs], [SMEM, VMEM, VMEM], after, out_specs=VMEM)


def spread(x, axis):
    return lax.all_to_all(x, axis, 0, 0, tiled=True)


def coeffs_kernel(where, *refs):
    sources, (out, grads, act, sems) = refs[:11], refs[11:]
    width = act.shape[-1] // 2
    copies = []
    for k, src in enumerate(sources[:7]):
        copies.append(pltpu.make_async_copy(src, act.at[k + (k >= 4)], sems.at[k]))
    for k, src in enumerate(sources[7:9]):
        copies.append(pltpu.make_async_copy(src, act.at[NZ // 2, :, :, :, pl.ds(k * width, width)], sems.at[7 + k]))
    for k, src in enumerate(sources[9:]):
        copies.append(pltpu.make_async_copy(src, grads.at[k], sems.at[9 + k]))
    for copy in copies:
        copy.start()
    for copy in copies:
        copy.wait()
    xh, c, z = where[0], where[1], where[2]
    total = None
    for seq in range(SEQS):
        left, right = [], []
        for block in (2 * seq, 2 * seq + 1):
            rel = lax.rem(block - z + NZ, NZ)
            for side in (0, 1):
                halved = lax.rem(rel, NZ // 2) == 0
                up = rel > NZ // 2
                core = jnp.where(halved, side, jnp.where(up, 0, 1))
                place = jnp.where(up, 2 * (NZ - rel) - 1 + side, 2 * rel - 1 + side)
                place = jnp.where(halved, 7 * (rel // (NZ // 2)), place)
                parity = jnp.bitwise_xor(jnp.bitwise_xor(xh, side), c)
                left += [act[rel, xh, parity], act[rel, 1 - xh, parity]]
                right.append(grads[jnp.bitwise_xor(core, c), place])
        coeffs = lax.dot_general(
            jnp.concatenate(left, axis=0),
            jnp.concatenate(right, axis=0),
            (((0,), (0,)), ((), ())),
            preferred_element_type=jnp.float32,
        )
        square = coeffs * coeffs
        total = square if total is None else total + square
    out[...] = total * (1.0 / SEQS)


def per_device(activations, grad_outputs, act_basis, grad_basis):
    z, xh, c = lax.axis_index("z"), lax.axis_index("xh"), lax.axis_index("c")
    where = jnp.stack([xh, c, z]).astype(jnp.int32)
    rows, half, width = grad_outputs.shape[0], grad_outputs.shape[0] // 2, grad_outputs.shape[1]
    cols = act_basis.shape[1]

    theirs = swap(grad_outputs, "xh")
    laps = [((grad_outputs, swap(grad_outputs, "c")), (theirs, swap(theirs, "c")))]
    for _ in range(3):
        laps.append(tuple(tuple(lap(x) for x in side) for side in laps[-1]))
    basis2 = swap(grad_basis, "c")

    act_x, act_basis2 = swap(activations, "xh"), swap(act_basis, "xh")
    act_copies = act_halves(where, activations, act_x, (laps[0][0][1],))
    (act_own,) = gate([spread(act_copies, CHIPS)], (*laps[2][0], act_basis2))
    act_oth = swap(act_own, "c")
    act_terms = rotate_act(act_own, act_oth, (act_basis, act_basis2))
    act_sum = lax.psum_scatter(act_terms.reshape(8 * rows, cols), "z", scatter_dimension=0, tiled=True)
    bases = grad_basis, basis2
    near = pick(where, list(zip(*laps[0])))
    early = rotate([near, laps[1][0], laps[1][1], laps[2][0], laps[2][1]], bases)
    far = [lap(x) for x in pick(where, list(zip(*laps[3])), (act_terms,))]
    terms = rotate([laps[3][0], laps[3][1], far], bases, (early,))

    parts = spread(terms, CHIPS)
    act_pair = summed(act_sum, 1, 1, (terms,))
    act_pair = jnp.concatenate([act_pair, swap(act_pair, "xh")], axis=0)
    one = hop(act_pair, act_pair)
    own = spread(summed(parts, 8, 8, one), CHIPS)
    two = hop(*one)
    three = hop(*two)
    four = hop(three[0][:, : cols // 2], three[1][:, cols // 2 :])
    (own,) = gate([own], four)
    other = swap(own, "c")

    acts = [x.reshape(2, 2, half, cols) for x in (act_pair, one[1], two[1], three[1], three[0], two[0], one[0])]
    acts += [x.reshape(2, 2, half, cols // 2) for x in four]
    return call(
        coeffs_kernel,
        jax.ShapeDtypeStruct((cols, width), jnp.float32),
        [where] + acts + [x.reshape(8, rows, width) for x in (own, other)],
        [SMEM] + [ANY] * 11,
        flops=703 * 10**6,
        moved=5 * 10**6,
        out_specs=VMEM,
        scratch_shapes=[
            pltpu.VMEM((2, 8, rows, width), jnp.bfloat16),
            pltpu.VMEM((NZ, 2, 2, half, cols), jnp.bfloat16),
            pltpu.SemaphoreType.DMA((11,)),
        ],
    )


def solution(mesh):
    fine = Mesh(mesh.devices.reshape(8, 2, 2, 4, 2), ("z", "xh", "xl", "y", "c"))
    return jax.shard_map(
        per_device,
        mesh=fine,
        in_specs=(P(NARROW, WIDE), P(WIDE, NARROW), P(WIDE, NARROW), P(NARROW, WIDE)),
        out_specs=P(NARROW, WIDE),
        check_vma=False,
    )
```

```python
import jax
import jax.numpy as jnp
from jax import lax
from jax.experimental import pallas as pl
from jax.experimental.pallas import tpu as pltpu
from jax.sharding import Mesh, PartitionSpec as P

SEQS = 4
NZ = 8
CHIPS, NARROW, WIDE = ("xl", "y"), ("xl", "y", "c"), ("z", "xh")


def shift(x, axis, by, size):
    return lax.ppermute(x, axis, [(i, (i + by) % size) for i in range(size)])


def swap(x, axis):
    return lax.ppermute(x, axis, [(0, 1), (1, 0)])


def dot(x, y):
    return jnp.dot(x, y, preferred_element_type=jnp.float32)


VMEM = pl.BlockSpec(memory_space=pltpu.VMEM)
ANY = pl.BlockSpec(memory_space=pl.ANY)
SMEM = pl.BlockSpec(memory_space=pltpu.SMEM)


def call(body, out, ins, specs, after=(), flops=10**6, moved=10**6, grant=16, **more):
    def kernel(*refs):
        body(*refs[: len(ins)], *refs[len(ins) + len(after) :])

    return pl.pallas_call(
        kernel,
        out_shape=out,
        in_specs=list(specs) + [ANY] * len(after),
        compiler_params=pltpu.CompilerParams(vmem_limit_bytes=grant * 1024 * 1024),
        cost_estimate=pl.CostEstimate(flops=flops, bytes_accessed=moved, transcendentals=0),
        **more,
    )(*ins, *after)


def gate(live, after=()):
    live = list(live)
    return call(
        lambda *refs: None,
        [jax.ShapeDtypeStruct(x.shape, x.dtype) for x in live],
        live,
        [VMEM] * len(live),
        after,
        out_specs=[VMEM] * len(live),
        input_output_aliases={k: k for k in range(len(live))},
    )


def hop(up, down):
    return shift(up, "z", 1, NZ), shift(down, "z", -1, NZ)


def lap(x, only=None):
    steps = [(z, c, (z + 1 - 2 * c) % NZ) for z in range(NZ) for c in (0, 1) if only in (None, c)]
    return lax.ppermute(x, ("z", "c"), [(2 * z + c, 2 * to + c) for z, c, to in steps])


def join(*arrays, cols=None, after=()):
    cols = [cols or x.shape[1] for x in arrays]

    def body(*refs):
        start = 0
        for ref, col in zip(refs, cols):
            refs[-1][:, start : start + col] = ref[:, :col]
            start += col

    out = jax.ShapeDtypeStruct((arrays[0].shape[0], sum(cols)), arrays[0].dtype)
    return call(body, out, arrays, [VMEM] * len(arrays), after, out_specs=VMEM)


def rotate(where, blocks, bases, done=(), after=()):
    parts = [block if isinstance(block, tuple) else (block,) for block in blocks]
    rows, depth, width = parts[0][0].shape[0], bases[0].shape[0], bases[0].shape[1]
    count, total = len(parts), sum(len(part) for part in parts)
    before = sum(x.shape[0] for x in done)

    def body(where, *refs):
        refs, bases, (*done, out, x, sems) = list(refs[:total]), refs[total : total + 2], refs[total + 2 :]
        copies = []
        for k, part in enumerate(parts):
            place, sem = x.at[pl.ds(k * rows, rows)], sems.at[k]
            copies.append(pltpu.make_async_copy(refs[0], place, sem))
            if len(part) == 1:
                copies[-1].start()
            else:
                for core in (0, 1):

                    @pl.when(where[1] == core)
                    def _():
                        pltpu.make_async_copy(refs[core], place, sem).start()

            refs = refs[len(part) :]
        for ref in done:
            out[:before] = ref[...]
        for copy in copies:
            copy.wait()
        out[before:] = (dot(x[:, :depth], bases[0][...]) + dot(x[:, depth:], bases[1][...])).astype(out.dtype)

    out = jax.ShapeDtypeStruct((before + count * rows, width), jnp.bfloat16)
    scratch = [
        pltpu.VMEM((count * rows, 2 * depth), jnp.bfloat16),
        pltpu.SemaphoreType.DMA((count,)),
    ]
    ins = [where, *(x for part in parts for x in part), *bases, *done]
    specs = [SMEM] + [ANY] * total + [VMEM] * (2 + len(done))
    flops = 4 * count * rows * depth * width
    return call(body, out, ins, specs, after, flops, 5 * 10**6, 52, out_specs=VMEM, scratch_shapes=scratch)


def summed(parts, count, copies, after=()):
    rows, width = parts.shape[0] // count, parts.shape[1]

    def body(x, out):
        total = x[:rows].astype(jnp.float32)
        for k in range(1, count):
            total = total + x[k * rows : (k + 1) * rows].astype(jnp.float32)
        total = total.astype(out.dtype)
        for k in range(copies):
            out[k * rows : (k + 1) * rows] = total

    out = jax.ShapeDtypeStruct((copies * rows, width), jnp.bfloat16)
    return call(body, out, [parts], [VMEM], after, out_specs=VMEM)


def rotate_act(own, other, bases, after=()):
    rows = own.shape[0] // 8
    depth, width = bases[0].shape

    def body(mine, theirs, first, second, out):
        for k, ref in enumerate((mine, theirs)):
            total = dot(ref[:, :depth], first[...]) + dot(ref[:, depth:], second[...])
            for chip in range(8):
                out[chip, k] = total[chip * rows : (chip + 1) * rows].astype(out.dtype)

    out = jax.ShapeDtypeStruct((8, 2, rows, width), jnp.bfloat16)
    return call(body, out, [own, other, *bases], [VMEM] * 4, after, 2 * 10**8, 2 * 10**6, out_specs=VMEM)


def act_halves(where, mine, theirs, after=()):
    half, depth = mine.shape[0] // 2, mine.shape[1]

    def body(where, mine, theirs, out):
        start = pl.multiple_of(where[0] * half, half)
        for k in range(8):
            out[k * half : (k + 1) * half, :depth] = mine[pl.ds(start, half)]
            out[k * half : (k + 1) * half, depth:] = theirs[pl.ds(start, half), -depth:]

    out = jax.ShapeDtypeStruct((8 * half, 2 * depth), mine.dtype)
    return call(body, out, [where, mine, theirs], [SMEM, VMEM, VMEM], after, out_specs=VMEM)


def spread(x, axis):
    return lax.all_to_all(x, axis, 0, 0, tiled=True)


def coeffs_kernel(where, *refs):
    sources, (out, grads, act, sems) = refs[:11], refs[11:]
    width = act.shape[-1] // 2
    copies = []
    for k, src in enumerate(sources[:7]):
        copies.append(pltpu.make_async_copy(src, act.at[k + (k >= 4)], sems.at[k]))
    for k, src in enumerate(sources[7:9]):
        copies.append(pltpu.make_async_copy(src, act.at[NZ // 2, :, :, :, pl.ds(k * width, width)], sems.at[7 + k]))
    for k, src in enumerate(sources[9:]):
        copies.append(pltpu.make_async_copy(src, grads.at[k], sems.at[9 + k]))
    for copy in copies:
        copy.start()
    for copy in copies:
        copy.wait()
    xh, c, z = where[0], where[1], where[2]
    total = None
    for seq in range(SEQS):
        left, right = [], []
        for block in (2 * seq, 2 * seq + 1):
            rel = lax.rem(block - z + NZ, NZ)
            for side in (0, 1):
                halved = lax.rem(rel, NZ // 2) == 0
                up = rel > NZ // 2
                core = jnp.where(halved, side, jnp.where(up, 0, 1))
                place = jnp.where(up, 2 * (NZ - rel) - 1 + side, 2 * rel - 1 + side)
                place = jnp.where(halved, 7 * (rel // (NZ // 2)), place)
                parity = jnp.bitwise_xor(jnp.bitwise_xor(xh, side), c)
                left += [act[rel, xh, parity], act[rel, 1 - xh, parity]]
                right.append(grads[jnp.bitwise_xor(core, c), place])
        coeffs = lax.dot_general(
            jnp.concatenate(left, axis=0),
            jnp.concatenate(right, axis=0),
            (((0,), (0,)), ((), ())),
            preferred_element_type=jnp.float32,
        )
        square = coeffs * coeffs
        total = square if total is None else total + square
    out[...] = total * (1.0 / SEQS)


def per_device(activations, grad_outputs, act_basis, grad_basis):
    z, xh, c = lax.axis_index("z"), lax.axis_index("xh"), lax.axis_index("c")
    where = jnp.stack([xh, c, z]).astype(jnp.int32)
    rows, half, width = grad_outputs.shape[0], grad_outputs.shape[0] // 2, grad_outputs.shape[1]
    cols = act_basis.shape[1]

    mate = swap(grad_outputs, "c")
    theirs = swap(join(grad_outputs, activations), "xh")
    act_basis2 = swap(act_basis, "xh")
    theirs_mate = swap(theirs, "c")
    act_copies = act_halves(where, activations, theirs, (mate, act_basis2))
    act_own = spread(act_copies, CHIPS)
    laps = [[join(grad_outputs, mate, after=(act_copies,)), join(theirs, theirs_mate, cols=width, after=(act_copies,))]]
    laps.append([lap(x) for x in laps[-1]])
    laps.append([lap(x) for x in laps[-1]])
    basis2 = swap(grad_basis, "c")
    (act_own,) = gate([act_own], (laps[1][0],))
    act_oth = swap(act_own, "c")
    act_terms = rotate_act(act_own, act_oth, (act_basis, act_basis2))
    act_parts = spread(act_terms.reshape(8 * rows, cols), "z")
    laps[2] = [*gate(laps[2][:1], (act_terms,)), laps[2][1]]
    laps.append([lap(x) for x in laps[-1]])
    bases = grad_basis, basis2
    early = rotate(where, [tuple(laps[0]), *laps[1], *laps[2]], bases)
    laps[3] = [*gate(laps[3][:1], (early,)), laps[3][1]]
    far = tuple(lap(x, core) for core, x in enumerate(laps[3]))
    act_half = summed(act_parts, 8, 1, laps[3][:1])
    act_mate = swap(act_half, "xh")
    terms = rotate(where, [*laps[3], far], bases, (early,), (act_mate,))
    parts = spread(terms, CHIPS)
    act_pair = jnp.concatenate([act_half, act_mate], axis=0)
    one = hop(act_pair, act_pair)
    two = hop(*one)
    three = hop(*two)
    four = hop(three[0][:, : cols // 2], three[1][:, cols // 2 :])
    own = spread(summed(parts, 8, 8, two), CHIPS)
    (own,) = gate([own], four)
    other = swap(own, "c")

    acts = [x.reshape(2, 2, half, cols) for x in (act_pair, one[1], two[1], three[1], three[0], two[0], one[0])]
    acts += [x.reshape(2, 2, half, cols // 2) for x in four]
    return call(
        coeffs_kernel,
        jax.ShapeDtypeStruct((cols, width), jnp.float32),
        [where] + acts + [x.reshape(8, rows, width) for x in (own, other)],
        [SMEM] + [ANY] * 11,
        flops=703 * 10**6,
        moved=5 * 10**6,
        out_specs=VMEM,
        scratch_shapes=[
            pltpu.VMEM((2, 8, rows, width), jnp.bfloat16),
            pltpu.VMEM((NZ, 2, 2, half, cols), jnp.bfloat16),
            pltpu.SemaphoreType.DMA((11,)),
        ],
    )


def solution(mesh):
    fine = Mesh(mesh.devices.reshape(8, 2, 2, 4, 2), ("z", "xh", "xl", "y", "c"))
    return jax.shard_map(
        per_device,
        mesh=fine,
        in_specs=(P(NARROW, WIDE), P(WIDE, NARROW), P(WIDE, NARROW), P(NARROW, WIDE)),
        out_specs=P(NARROW, WIDE),
        check_vma=False,
    )
```

```python
import jax
import jax.numpy as jnp
from jax import lax
from jax.experimental import pallas as pl
from jax.experimental.pallas import tpu as pltpu
from jax.sharding import Mesh, PartitionSpec as P

SEQS = 4
NZ = 8
CHIPS, NARROW, WIDE = ("xl", "y"), ("xl", "y", "c"), ("z", "xh")


def shift(x, axis, by, size):
    return lax.ppermute(x, axis, [(i, (i + by) % size) for i in range(size)])


def swap(x, axis):
    return lax.ppermute(x, axis, [(0, 1), (1, 0)])


def dot(x, y):
    return jnp.dot(x, y, preferred_element_type=jnp.float32)


VMEM = pl.BlockSpec(memory_space=pltpu.VMEM)
ANY = pl.BlockSpec(memory_space=pl.ANY)
SMEM = pl.BlockSpec(memory_space=pltpu.SMEM)


def call(body, out, ins, specs, after=(), flops=10**6, moved=10**6, grant=16, **more):
    def kernel(*refs):
        body(*refs[: len(ins)], *refs[len(ins) + len(after) :])

    return pl.pallas_call(
        kernel,
        out_shape=out,
        in_specs=list(specs) + [ANY] * len(after),
        compiler_params=pltpu.CompilerParams(vmem_limit_bytes=grant * 1024 * 1024),
        cost_estimate=pl.CostEstimate(flops=flops, bytes_accessed=moved, transcendentals=0),
        **more,
    )(*ins, *after)


def gate(live, after=()):
    live = list(live)
    return call(
        lambda *refs: None,
        [jax.ShapeDtypeStruct(x.shape, x.dtype) for x in live],
        live,
        [VMEM] * len(live),
        after,
        out_specs=[VMEM] * len(live),
        input_output_aliases={k: k for k in range(len(live))},
    )


def hop(up, down, by=1):
    return shift(up, "z", by, NZ), shift(down, "z", -by, NZ)


def lap(x, only=None):
    steps = [(z, c, (z + 1 - 2 * c) % NZ) for z in range(NZ) for c in (0, 1) if only in (None, c)]
    return lax.ppermute(x, ("z", "c"), [(2 * z + c, 2 * to + c) for z, c, to in steps])


def join(*arrays, cols=None, after=()):
    cols = [cols or x.shape[1] for x in arrays]

    def body(*refs):
        start = 0
        for ref, col in zip(refs, cols):
            refs[-1][:, start : start + col] = ref[:, :col]
            start += col

    out = jax.ShapeDtypeStruct((arrays[0].shape[0], sum(cols)), arrays[0].dtype)
    return call(body, out, arrays, [VMEM] * len(arrays), after, out_specs=VMEM)


def rotate(where, blocks, bases, start, total, sums=(), after=()):
    parts = [block if isinstance(block, tuple) else (block,) for block in blocks]
    rows, depth, width = parts[0][0].shape[0], bases[0].shape[0], bases[0].shape[1]
    count, many = len(parts), sum(len(part) for part in parts)

    def body(where, *refs):
        refs, bases, (out, token, x, base, result, sems, out_sems, base_sems) = list(refs[:many]), refs[many : many + 2], refs[-8:]
        copies, slab = [], depth // 7
        for k in range(14):
            source = bases[k // 7].at[pl.ds(k % 7 * slab, slab)]
            copies.append(pltpu.make_async_copy(source, base.at[pl.ds(k * slab, slab)], base_sems.at[k]))
            copies[-1].start()
        for k, part in enumerate(parts):
            place, sem = x.at[pl.ds(k * rows, rows)], sems.at[k]
            copies.append(pltpu.make_async_copy(refs[0], place, sem))
            if len(part) == 1:
                copies[-1].start()
            else:
                for core in (0, 1):

                    @pl.when(where[1] == core)
                    def _():
                        pltpu.make_async_copy(refs[core], place, sem).start()

            refs = refs[len(part) :]
        for copy in copies:
            copy.wait()
        result[...] = dot(x[...], base[...]).astype(result.dtype)
        token[...] = jnp.zeros_like(token)
        copies = []
        for k in range(count):
            here, there = pl.ds(k * rows, rows), pl.ds(start + k * rows, rows)
            copies.append(pltpu.make_async_copy(result.at[here], out.at[there], out_sems.at[k]))
            copies[-1].start()
        for copy in copies:
            copy.wait()

    out = [jax.ShapeDtypeStruct((total, width), jnp.bfloat16), jax.ShapeDtypeStruct((8, 128), jnp.float32)]
    scratch = [
        pltpu.VMEM((count * rows, 2 * depth), jnp.bfloat16),
        pltpu.VMEM((2 * depth, width), jnp.bfloat16),
        pltpu.VMEM((count * rows, width), jnp.bfloat16),
        pltpu.SemaphoreType.DMA((count,)),
        pltpu.SemaphoreType.DMA((count,)),
        pltpu.SemaphoreType.DMA((14,)),
    ]
    ins = [where, *(x for part in parts for x in part), *bases, *sums]
    specs = [SMEM] + [ANY] * (len(ins) - 1)
    flops = 4 * count * rows * depth * width
    more = {"input_output_aliases": {len(ins) - 1: 0}} if sums else {}
    return call(body, out, ins, specs, after, flops, 5 * 10**6, 52, out_specs=[ANY, VMEM], scratch_shapes=scratch, **more)


def summed(parts, count, copies, after=()):
    rows, width = parts.shape[0] // count, parts.shape[1]

    def body(x, out):
        total = x[:rows].astype(jnp.float32)
        for k in range(1, count):
            total = total + x[k * rows : (k + 1) * rows].astype(jnp.float32)
        total = total.astype(out.dtype)
        for k in range(copies):
            out[k * rows : (k + 1) * rows] = total

    out = jax.ShapeDtypeStruct((copies * rows, width), jnp.bfloat16)
    return call(body, out, [parts], [VMEM], after, out_specs=VMEM)


def rotate_act(own, other, bases, after=()):
    rows = own.shape[0] // 8
    depth, width = bases[0].shape

    def body(mine, theirs, first, second, out):
        for k, ref in enumerate((mine, theirs)):
            total = dot(ref[:, :depth], first[...]) + dot(ref[:, depth:], second[...])
            for chip in range(8):
                out[chip, k] = total[chip * rows : (chip + 1) * rows].astype(out.dtype)

    out = jax.ShapeDtypeStruct((8, 2, rows, width), jnp.bfloat16)
    return call(body, out, [own, other, *bases], [VMEM] * 4, after, 2 * 10**8, 2 * 10**6, out_specs=VMEM)


def act_halves(where, mine, theirs, after=()):
    half, depth = mine.shape[0] // 2, mine.shape[1]

    def body(where, mine, theirs, out):
        start = pl.multiple_of(where[0] * half, half)
        for k in range(8):
            out[k * half : (k + 1) * half, :depth] = mine[pl.ds(start, half)]
            out[k * half : (k + 1) * half, depth:] = theirs[pl.ds(start, half), -depth:]

    out = jax.ShapeDtypeStruct((8 * half, 2 * depth), mine.dtype)
    return call(body, out, [where, mine, theirs], [SMEM, VMEM, VMEM], after, out_specs=VMEM)


def spread(x, axis):
    return lax.all_to_all(x, axis, 0, 0, tiled=True)


def coeffs_kernel(where, *refs):
    sources, (mine, other, out, act) = refs[:9], refs[9:]
    width = act.shape[-1] // 2
    for k, src in enumerate(sources[:7]):
        act[k + (k >= 4)] = src[...]
    for k, src in enumerate(sources[7:]):
        act[NZ // 2, :, :, :, k * width : (k + 1) * width] = src[...]
    xh, c, z = where[0], where[1], where[2]
    total = None
    for seq in range(SEQS):
        left, right = [], []
        for block in (2 * seq, 2 * seq + 1):
            rel = lax.rem(block - z + NZ, NZ)
            for side in (0, 1):
                halved = lax.rem(rel, NZ // 2) == 0
                up = rel > NZ // 2
                core = jnp.where(halved, side, jnp.where(up, 0, 1))
                place = jnp.where(up, 2 * (NZ - rel) - 1 + side, 2 * rel - 1 + side)
                place = jnp.where(halved, 7 * (rel // (NZ // 2)), place)
                parity = jnp.bitwise_xor(jnp.bitwise_xor(xh, side), c)
                left += [act[rel, xh, parity], act[rel, 1 - xh, parity]]
                right.append(jnp.where(core == c, mine[place], other[place]))
        coeffs = lax.dot_general(
            jnp.concatenate(left, axis=0),
            jnp.concatenate(right, axis=0),
            (((0,), (0,)), ((), ())),
            preferred_element_type=jnp.float32,
        )
        square = coeffs * coeffs
        total = square if total is None else total + square
    out[...] = total * (1.0 / SEQS)


def per_device(activations, grad_outputs, act_basis, grad_basis):
    z, xh, c = lax.axis_index("z"), lax.axis_index("xh"), lax.axis_index("c")
    where = jnp.stack([xh, c, z]).astype(jnp.int32)
    rows, half, width = grad_outputs.shape[0], grad_outputs.shape[0] // 2, grad_outputs.shape[1]
    cols = act_basis.shape[1]

    mate = swap(grad_outputs, "c")
    theirs = swap(join(grad_outputs, activations), "xh")
    act_basis2 = swap(act_basis, "xh")
    theirs_mate = swap(theirs, "c")
    act_copies = act_halves(where, activations, theirs, (mate,))
    act_own = spread(act_copies, CHIPS)
    laps = [[join(grad_outputs, mate, after=(act_copies,)), join(theirs, theirs_mate, cols=width, after=(act_copies,))]]
    laps.append([lap(x) for x in laps[-1]])
    laps.append([lap(x) for x in laps[-1]])
    basis2 = swap(grad_basis, "c")
    (act_own,) = gate([act_own], (laps[1][0], act_basis2))
    act_oth = swap(act_own, "c")
    act_terms = rotate_act(act_own, act_oth, (act_basis, act_basis2))
    act_parts = spread(act_terms.reshape(8 * rows, cols), "z")
    laps[2] = [*gate(laps[2][:1], (act_terms,)), laps[2][1]]
    laps.append([lap(x) for x in laps[-1]])
    bases = grad_basis, basis2
    early, token = rotate(where, [tuple(laps[0]), *laps[1], *laps[2]], bases, 0, 8 * rows)
    laps[3] = [*gate(laps[3][:1], (token,)), laps[3][1]]
    far = tuple(lap(x, core) for core, x in enumerate(laps[3]))
    act_half = summed(act_parts, 8, 1, laps[3][:1])
    act_mate = swap(act_half, "xh")
    terms, _ = rotate(where, [*laps[3], far], bases, 5 * rows, 8 * rows, (early,), (act_mate,))
    parts = spread(terms, CHIPS)
    act_pair = jnp.concatenate([act_half, act_mate], axis=0)
    one = hop(act_pair, act_pair)
    two = hop(act_pair, act_pair, 2)
    own = spread(summed(parts, 8, 8, one + two), CHIPS)
    three = hop(*two)
    four = hop(two[0][:, : cols // 2], two[1][:, cols // 2 :], 2)
    (own,) = gate([own], three + four)
    other = swap(own, "c")

    acts = [x.reshape(2, 2, half, cols) for x in (act_pair, one[1], two[1], three[1], three[0], two[0], one[0])]
    acts += [x.reshape(2, 2, half, cols // 2) for x in four]
    return call(
        coeffs_kernel,
        jax.ShapeDtypeStruct((cols, width), jnp.float32),
        [where] + acts + [x.reshape(8, rows, width) for x in (own, other)],
        [SMEM] + [VMEM] * 11,
        flops=703 * 10**6,
        moved=5 * 10**6,
        out_specs=VMEM,
        scratch_shapes=[
            pltpu.VMEM((NZ, 2, 2, half, cols), jnp.bfloat16),
        ],
    )


def solution(mesh):
    fine = Mesh(mesh.devices.reshape(8, 2, 2, 4, 2), ("z", "xh", "xl", "y", "c"))
    return jax.shard_map(
        per_device,
        mesh=fine,
        in_specs=(P(NARROW, WIDE), P(WIDE, NARROW), P(WIDE, NARROW), P(NARROW, WIDE)),
        out_specs=P(NARROW, WIDE),
        check_vma=False,
    )
```

```python
import jax
import jax.numpy as jnp
from jax import lax
from jax.experimental import pallas as pl
from jax.experimental.pallas import tpu as pltpu
from jax.sharding import Mesh, PartitionSpec as P

SEQS = 4
NZ = 8
CHIPS, NARROW, WIDE = ("xl", "y"), ("xl", "y", "c"), ("z", "xh")


def shift(x, axis, by, size):
    return lax.ppermute(x, axis, [(i, (i + by) % size) for i in range(size)])


def swap(x, axis):
    return lax.ppermute(x, axis, [(0, 1), (1, 0)])


def dot(x, y):
    return jnp.dot(x, y, preferred_element_type=jnp.float32)


VMEM = pl.BlockSpec(memory_space=pltpu.VMEM)
ANY = pl.BlockSpec(memory_space=pl.ANY)
SMEM = pl.BlockSpec(memory_space=pltpu.SMEM)


def call(body, out, ins, specs, after=(), flops=10**6, moved=10**6, grant=16, **more):
    def kernel(*refs):
        body(*refs[: len(ins)], *refs[len(ins) + len(after) :])

    return pl.pallas_call(
        kernel,
        out_shape=out,
        in_specs=list(specs) + [ANY] * len(after),
        compiler_params=pltpu.CompilerParams(vmem_limit_bytes=grant * 1024 * 1024),
        cost_estimate=pl.CostEstimate(flops=flops, bytes_accessed=moved, transcendentals=0),
        **more,
    )(*ins, *after)


def gate(live, after=()):
    live = list(live)
    return call(
        lambda *refs: None,
        [jax.ShapeDtypeStruct(x.shape, x.dtype) for x in live],
        live,
        [VMEM] * len(live),
        after,
        out_specs=[VMEM] * len(live),
        input_output_aliases={k: k for k in range(len(live))},
    )


def hop(up, down, by=1):
    return shift(up, "z", by, NZ), shift(down, "z", -by, NZ)


def lap(x, only=None):
    steps = [(z, c, (z + 1 - 2 * c) % NZ) for z in range(NZ) for c in (0, 1) if only in (None, c)]
    return lax.ppermute(x, ("z", "c"), [(2 * z + c, 2 * to + c) for z, c, to in steps])


def join(*arrays, cols=None, after=()):
    cols = [cols or x.shape[1] for x in arrays]

    def body(*refs):
        start = 0
        for ref, col in zip(refs, cols):
            refs[-1][:, start : start + col] = ref[:, :col]
            start += col

    out = jax.ShapeDtypeStruct((arrays[0].shape[0], sum(cols)), arrays[0].dtype)
    return call(body, out, arrays, [VMEM] * len(arrays), after, out_specs=VMEM)


def rotate(where, blocks, bases, start, total, sums=(), after=(), fetch=True):
    parts = [block if isinstance(block, tuple) else (block,) for block in blocks]
    rows, depth, width = parts[0][0].shape[0], bases[0].shape[0], bases[0].shape[1]
    count, many = len(parts), sum(len(part) for part in parts)

    def body(where, *refs):
        refs, bases, (out, token, x, base, result, sems, out_sems, base_sems) = list(refs[:many]), refs[many : many + 2], refs[-8:]
        copies, slab = [], depth // 7
        for k in range(14 if fetch else 0):
            source = bases[k // 7].at[pl.ds(k % 7 * slab, slab)]
            copies.append(pltpu.make_async_copy(source, base.at[pl.ds(k * slab, slab)], base_sems.at[k]))
            copies[-1].start()
        for k, part in enumerate(parts):
            place, sem = x.at[pl.ds(k * rows, rows)], sems.at[k]
            copies.append(pltpu.make_async_copy(refs[0], place, sem))
            if len(part) == 1:
                copies[-1].start()
            else:
                for core in (0, 1):

                    @pl.when(where[1] == core)
                    def _():
                        pltpu.make_async_copy(refs[core], place, sem).start()

            refs = refs[len(part) :]
        for copy in copies:
            copy.wait()
        first, second = (base[:depth], base[depth:]) if fetch else (bases[0][...], bases[1][...])
        result[...] = (dot(x[:, :depth], first) + dot(x[:, depth:], second)).astype(result.dtype)
        token[...] = jnp.zeros_like(token)
        copies = []
        for k in range(count):
            here, there = pl.ds(k * rows, rows), pl.ds(start + k * rows, rows)
            copies.append(pltpu.make_async_copy(result.at[here], out.at[there], out_sems.at[k]))
            copies[-1].start()
        for copy in copies:
            copy.wait()

    out = [jax.ShapeDtypeStruct((total, width), jnp.bfloat16), jax.ShapeDtypeStruct((8, 128), jnp.float32)]
    scratch = [
        pltpu.VMEM((count * rows, 2 * depth), jnp.bfloat16),
        pltpu.VMEM((2 * depth if fetch else 16, width), jnp.bfloat16),
        pltpu.VMEM((count * rows, width), jnp.bfloat16),
        pltpu.SemaphoreType.DMA((count,)),
        pltpu.SemaphoreType.DMA((count,)),
        pltpu.SemaphoreType.DMA((14,)),
    ]
    ins = [where, *(x for part in parts for x in part), *bases, *sums]
    specs = [SMEM] + [ANY] * many + [ANY if fetch else VMEM] * 2 + [ANY] * len(sums)
    flops = 4 * count * rows * depth * width
    more = {"input_output_aliases": {len(ins) - 1: 0}} if sums else {}
    return call(body, out, ins, specs, after, flops, 5 * 10**6, 52, out_specs=[ANY, VMEM], scratch_shapes=scratch, **more)


def summed(parts, count, copies, after=()):
    rows, width = parts.shape[0] // count, parts.shape[1]

    def body(x, out):
        total = x[:rows].astype(jnp.float32)
        for k in range(1, count):
            total = total + x[k * rows : (k + 1) * rows].astype(jnp.float32)
        total = total.astype(out.dtype)
        for k in range(copies):
            out[k * rows : (k + 1) * rows] = total

    out = jax.ShapeDtypeStruct((copies * rows, width), jnp.bfloat16)
    return call(body, out, [parts], [VMEM], after, out_specs=VMEM)


def rotate_act(own, other, bases, after=()):
    rows = own.shape[0] // 8
    depth, width = bases[0].shape

    def body(mine, theirs, first, second, out):
        for k, ref in enumerate((mine, theirs)):
            total = dot(ref[:, :depth], first[...]) + dot(ref[:, depth:], second[...])
            for chip in range(8):
                out[chip, k] = total[chip * rows : (chip + 1) * rows].astype(out.dtype)

    out = jax.ShapeDtypeStruct((8, 2, rows, width), jnp.bfloat16)
    return call(body, out, [own, other, *bases], [VMEM] * 4, after, 2 * 10**8, 2 * 10**6, out_specs=VMEM)


def act_halves(where, mine, theirs, depth, after=()):
    half, width = mine.shape[0] // 2, mine.shape[1]

    def body(where, mine, theirs, out):
        start = pl.multiple_of(where[0] * half, half)
        for k in range(8):
            out[k * half : (k + 1) * half, :depth] = mine[pl.ds(start, half), width - depth :]
            out[k * half : (k + 1) * half, depth:] = theirs[pl.ds(start, half), width - depth :]

    out = jax.ShapeDtypeStruct((8 * half, 2 * depth), mine.dtype)
    return call(body, out, [where, mine, theirs], [SMEM, VMEM, VMEM], after, out_specs=VMEM)


def spread(x, axis):
    return lax.all_to_all(x, axis, 0, 0, tiled=True)


def coeffs_kernel(where, *refs):
    sources, (mine, other, out, act) = refs[:9], refs[9:]
    width = act.shape[-1] // 2
    for k, src in enumerate(sources[:7]):
        act[k + (k >= 4)] = src[...]
    for k, src in enumerate(sources[7:]):
        act[NZ // 2, :, :, :, k * width : (k + 1) * width] = src[...]
    xh, c, z = where[0], where[1], where[2]
    total = None
    for seq in range(SEQS):
        left, right = [], []
        for block in (2 * seq, 2 * seq + 1):
            rel = lax.rem(block - z + NZ, NZ)
            for side in (0, 1):
                halved = lax.rem(rel, NZ // 2) == 0
                up = rel > NZ // 2
                core = jnp.where(halved, side, jnp.where(up, 0, 1))
                place = jnp.where(up, 2 * (NZ - rel) - 1 + side, 2 * rel - 1 + side)
                place = jnp.where(halved, 7 * (rel // (NZ // 2)), place)
                parity = jnp.bitwise_xor(jnp.bitwise_xor(xh, side), c)
                left += [act[rel, xh, parity], act[rel, 1 - xh, parity]]
                right.append(jnp.where(core == c, mine[place], other[place]))
        coeffs = lax.dot_general(
            jnp.concatenate(left, axis=0),
            jnp.concatenate(right, axis=0),
            (((0,), (0,)), ((), ())),
            preferred_element_type=jnp.float32,
        )
        square = coeffs * coeffs
        total = square if total is None else total + square
    out[...] = total * (1.0 / SEQS)


def per_device(activations, grad_outputs, act_basis, grad_basis):
    z, xh, c = lax.axis_index("z"), lax.axis_index("xh"), lax.axis_index("c")
    where = jnp.stack([xh, c, z]).astype(jnp.int32)
    rows, half, width = grad_outputs.shape[0], grad_outputs.shape[0] // 2, grad_outputs.shape[1]
    cols = act_basis.shape[1]

    mate = swap(grad_outputs, "c")
    mine = join(grad_outputs, activations)
    theirs = swap(mine, "xh")
    act_basis2 = swap(act_basis, "xh")
    theirs_mate = swap(theirs, "c")
    act_copies = act_halves(where, mine, theirs, activations.shape[1])
    act_own = spread(act_copies, CHIPS)
    laps = [[join(grad_outputs, mate, after=(act_copies,)), join(theirs, theirs_mate, cols=width, after=(act_copies,))]]
    laps.append([lap(x) for x in laps[-1]])
    laps.append([lap(x) for x in laps[-1]])
    basis2 = swap(grad_basis, "c")
    (act_own,) = gate([act_own], (laps[1][0], act_basis2))
    act_oth = swap(act_own, "c")
    act_terms = rotate_act(act_own, act_oth, (act_basis, act_basis2))
    act_parts = spread(act_terms.reshape(8 * rows, cols), "z")
    laps[2] = [*gate(laps[2][:1], (act_terms,)), laps[2][1]]
    laps.append([lap(x) for x in laps[-1]])
    bases = grad_basis, basis2
    early, token = rotate(where, [tuple(laps[0]), *laps[1], *laps[2]], bases, 0, 8 * rows)
    laps[3] = [*gate(laps[3][:1], (token,)), laps[3][1]]
    far = tuple(lap(x, core) for core, x in enumerate(laps[3]))
    act_half = summed(act_parts, 8, 1, laps[3][:1])
    act_mate = swap(act_half, "xh")
    terms, _ = rotate(where, [*laps[3], far], bases, 5 * rows, 8 * rows, (early,), (act_mate,), False)
    parts = spread(terms, CHIPS)
    act_pair = jnp.concatenate([act_half, act_mate], axis=0)
    one = hop(act_pair, act_pair)
    two = hop(act_pair, act_pair, 2)
    own = spread(summed(parts, 8, 8, one + two), CHIPS)
    three = hop(*two)
    four = hop(two[0][:, : cols // 2], two[1][:, cols // 2 :], 2)
    (own,) = gate([own], three + four)
    other = swap(own, "c")

    acts = [x.reshape(2, 2, half, cols) for x in (act_pair, one[1], two[1], three[1], three[0], two[0], one[0])]
    acts += [x.reshape(2, 2, half, cols // 2) for x in four]
    return call(
        coeffs_kernel,
        jax.ShapeDtypeStruct((cols, width), jnp.float32),
        [where] + acts + [x.reshape(8, rows, width) for x in (own, other)],
        [SMEM] + [VMEM] * 11,
        flops=703 * 10**6,
        moved=5 * 10**6,
        out_specs=VMEM,
        scratch_shapes=[
            pltpu.VMEM((NZ, 2, 2, half, cols), jnp.bfloat16),
        ],
    )


def solution(mesh):
    fine = Mesh(mesh.devices.reshape(8, 2, 2, 4, 2), ("z", "xh", "xl", "y", "c"))
    return jax.shard_map(
        per_device,
        mesh=fine,
        in_specs=(P(NARROW, WIDE), P(WIDE, NARROW), P(WIDE, NARROW), P(NARROW, WIDE)),
        out_specs=P(NARROW, WIDE),
        check_vma=False,
    )
```

```python
import jax
import jax.numpy as jnp
from jax import lax
from jax.experimental import pallas as pl
from jax.experimental.pallas import tpu as pltpu
from jax.sharding import Mesh, PartitionSpec as P

SEQS = 4
NZ = 8
CHIPS, NARROW, WIDE = ("xl", "y"), ("xl", "y", "c"), ("z", "xh")


def shift(x, axis, by, size):
    return lax.ppermute(x, axis, [(i, (i + by) % size) for i in range(size)])


def swap(x, axis):
    return lax.ppermute(x, axis, [(0, 1), (1, 0)])


def dot(x, y):
    return jnp.dot(x, y, preferred_element_type=jnp.float32)


VMEM = pl.BlockSpec(memory_space=pltpu.VMEM)
ANY = pl.BlockSpec(memory_space=pl.ANY)
SMEM = pl.BlockSpec(memory_space=pltpu.SMEM)


def call(body, out, ins, specs, after=(), flops=10**6, moved=10**6, grant=16, **more):
    def kernel(*refs):
        body(*refs[: len(ins)], *refs[len(ins) + len(after) :])

    return pl.pallas_call(
        kernel,
        out_shape=out,
        in_specs=list(specs) + [ANY] * len(after),
        compiler_params=pltpu.CompilerParams(vmem_limit_bytes=grant * 1024 * 1024),
        cost_estimate=pl.CostEstimate(flops=flops, bytes_accessed=moved, transcendentals=0),
        **more,
    )(*ins, *after)


def gate(live, after=()):
    live = list(live)
    return call(
        lambda *refs: None,
        [jax.ShapeDtypeStruct(x.shape, x.dtype) for x in live],
        live,
        [VMEM] * len(live),
        after,
        out_specs=[VMEM] * len(live),
        input_output_aliases={k: k for k in range(len(live))},
    )


def hop(up, down, by=1):
    return shift(up, "z", by, NZ), shift(down, "z", -by, NZ)


def lap(x, only=None):
    steps = [(z, c, (z + 1 - 2 * c) % NZ) for z in range(NZ) for c in (0, 1) if only in (None, c)]
    return lax.ppermute(x, ("z", "c"), [(2 * z + c, 2 * to + c) for z, c, to in steps])


def join(*arrays, cols=None, after=()):
    cols = [cols or x.shape[1] for x in arrays]

    def body(*refs):
        start = 0
        for ref, col in zip(refs, cols):
            refs[-1][:, start : start + col] = ref[:, :col]
            start += col

    out = jax.ShapeDtypeStruct((arrays[0].shape[0], sum(cols)), arrays[0].dtype)
    return call(body, out, arrays, [VMEM] * len(arrays), after, out_specs=VMEM)


def rotate(where, blocks, bases, start, total, sums=(), after=()):
    parts = [block if isinstance(block, tuple) else (block,) for block in blocks]
    rows, depth, width = parts[0][0].shape[0], bases[0].shape[0], bases[0].shape[1]
    count, many = len(parts), sum(len(part) for part in parts)

    def body(where, *refs):
        refs, bases, (out, token, x, base, result, sems, out_sems, base_sems) = list(refs[:many]), refs[many : many + 2], refs[-8:]
        copies, slab = [], depth // 7
        for k in range(14):
            source = bases[k // 7].at[pl.ds(k % 7 * slab, slab)]
            copies.append(pltpu.make_async_copy(source, base.at[pl.ds(k * slab, slab)], base_sems.at[k]))
            copies[-1].start()
        for k, part in enumerate(parts):
            place, sem = x.at[pl.ds(k * rows, rows)], sems.at[k]
            copies.append(pltpu.make_async_copy(refs[0], place, sem))
            if len(part) == 1:
                copies[-1].start()
            else:
                for core in (0, 1):

                    @pl.when(where[1] == core)
                    def _():
                        pltpu.make_async_copy(refs[core], place, sem).start()

            refs = refs[len(part) :]
        for copy in copies[:7] + copies[14:]:
            copy.wait()
        total_first = dot(x[:, :depth], base[:depth])
        for copy in copies[7:14]:
            copy.wait()
        result[...] = (total_first + dot(x[:, depth:], base[depth:])).astype(result.dtype)
        token[...] = jnp.zeros_like(token)
        copies = []
        for k in range(count):
            here, there = pl.ds(k * rows, rows), pl.ds(start + k * rows, rows)
            copies.append(pltpu.make_async_copy(result.at[here], out.at[there], out_sems.at[k]))
            copies[-1].start()
        for copy in copies:
            copy.wait()

    out = [jax.ShapeDtypeStruct((total, width), jnp.bfloat16), jax.ShapeDtypeStruct((8, 128), jnp.float32)]
    scratch = [
        pltpu.VMEM((count * rows, 2 * depth), jnp.bfloat16),
        pltpu.VMEM((2 * depth, width), jnp.bfloat16),
        pltpu.VMEM((count * rows, width), jnp.bfloat16),
        pltpu.SemaphoreType.DMA((count,)),
        pltpu.SemaphoreType.DMA((count,)),
        pltpu.SemaphoreType.DMA((14,)),
    ]
    ins = [where, *(x for part in parts for x in part), *bases, *sums]
    specs = [SMEM] + [ANY] * (len(ins) - 1)
    flops = 4 * count * rows * depth * width
    more = {"input_output_aliases": {len(ins) - 1: 0}} if sums else {}
    return call(body, out, ins, specs, after, flops, 5 * 10**6, 52, out_specs=[ANY, VMEM], scratch_shapes=scratch, **more)


def summed(parts, count, copies, after=()):
    rows, width = parts.shape[0] // count, parts.shape[1]

    def body(x, out):
        total = x[:rows].astype(jnp.float32)
        for k in range(1, count):
            total = total + x[k * rows : (k + 1) * rows].astype(jnp.float32)
        total = total.astype(out.dtype)
        for k in range(copies):
            out[k * rows : (k + 1) * rows] = total

    out = jax.ShapeDtypeStruct((copies * rows, width), jnp.bfloat16)
    return call(body, out, [parts], [VMEM], after, out_specs=VMEM)


def rotate_act(own, other, bases, after=()):
    rows = own.shape[0] // 8
    depth, width = bases[0].shape

    def body(mine, theirs, first, second, out):
        for k, ref in enumerate((mine, theirs)):
            total = dot(ref[:, :depth], first[...]) + dot(ref[:, depth:], second[...])
            for chip in range(8):
                out[chip, k] = total[chip * rows : (chip + 1) * rows].astype(out.dtype)

    out = jax.ShapeDtypeStruct((8, 2, rows, width), jnp.bfloat16)
    return call(body, out, [own, other, *bases], [VMEM] * 4, after, 2 * 10**8, 2 * 10**6, out_specs=VMEM)


def act_halves(where, mine, theirs, depth, after=()):
    half, width = mine.shape[0] // 2, mine.shape[1]

    def body(where, mine, theirs, out):
        start = pl.multiple_of(where[0] * half, half)
        for k in range(8):
            out[k * half : (k + 1) * half, :depth] = mine[pl.ds(start, half), width - depth :]
            out[k * half : (k + 1) * half, depth:] = theirs[pl.ds(start, half), width - depth :]

    out = jax.ShapeDtypeStruct((8 * half, 2 * depth), mine.dtype)
    return call(body, out, [where, mine, theirs], [SMEM, VMEM, VMEM], after, out_specs=VMEM)


def spread(x, axis):
    return lax.all_to_all(x, axis, 0, 0, tiled=True)


def coeffs_kernel(where, *refs):
    sources, (mine, other, out, act) = refs[:9], refs[9:]
    width = act.shape[-1] // 2
    for k, src in enumerate(sources[:7]):
        act[k + (k >= 4)] = src[...]
    for k, src in enumerate(sources[7:]):
        act[NZ // 2, :, :, :, k * width : (k + 1) * width] = src[...]
    xh, c, z = where[0], where[1], where[2]
    total = None
    for seq in range(SEQS):
        left, right = [], []
        for block in (2 * seq, 2 * seq + 1):
            rel = lax.rem(block - z + NZ, NZ)
            for side in (0, 1):
                halved = lax.rem(rel, NZ // 2) == 0
                up = rel > NZ // 2
                core = jnp.where(halved, side, jnp.where(up, 0, 1))
                place = jnp.where(up, 2 * (NZ - rel) - 1 + side, 2 * rel - 1 + side)
                place = jnp.where(halved, 7 * (rel // (NZ // 2)), place)
                parity = jnp.bitwise_xor(jnp.bitwise_xor(xh, side), c)
                left += [act[rel, xh, parity], act[rel, 1 - xh, parity]]
                right.append(jnp.where(core == c, mine[place], other[place]))
        coeffs = lax.dot_general(
            jnp.concatenate(left, axis=0),
            jnp.concatenate(right, axis=0),
            (((0,), (0,)), ((), ())),
            preferred_element_type=jnp.float32,
        )
        square = coeffs * coeffs
        total = square if total is None else total + square
    out[...] = total * (1.0 / SEQS)


def per_device(activations, grad_outputs, act_basis, grad_basis):
    z, xh, c = lax.axis_index("z"), lax.axis_index("xh"), lax.axis_index("c")
    where = jnp.stack([xh, c, z]).astype(jnp.int32)
    rows, half, width = grad_outputs.shape[0], grad_outputs.shape[0] // 2, grad_outputs.shape[1]
    cols = act_basis.shape[1]

    mate = swap(grad_outputs, "c")
    mine = join(grad_outputs, activations)
    theirs = swap(mine, "xh")
    act_basis2 = swap(act_basis, "xh")
    theirs_mate = swap(theirs, "c")
    act_copies = act_halves(where, mine, theirs, activations.shape[1])
    act_own = spread(act_copies, CHIPS)
    laps = [[join(grad_outputs, mate, after=(act_copies,)), join(theirs, theirs_mate, cols=width, after=(act_copies,))]]
    laps.append([lap(x) for x in laps[-1]])
    laps.append([lap(x) for x in laps[-1]])
    basis2 = swap(grad_basis, "c")
    (act_own,) = gate([act_own], (laps[1][0], act_basis2))
    act_oth = swap(act_own, "c")
    act_terms = rotate_act(act_own, act_oth, (act_basis, act_basis2))
    act_parts = spread(act_terms.reshape(8 * rows, cols), "z")
    laps[2] = [*gate(laps[2][:1], (act_terms,)), laps[2][1]]
    laps.append([lap(x) for x in laps[-1]])
    bases = grad_basis, basis2
    early, token = rotate(where, [tuple(laps[0]), *laps[1], *laps[2]], bases, 0, 8 * rows)
    laps[3] = [*gate(laps[3][:1], (token,)), laps[3][1]]
    far = tuple(lap(x, core) for core, x in enumerate(laps[3]))
    act_half = summed(act_parts, 8, 1, laps[3][:1])
    act_mate = swap(act_half, "xh")
    terms, _ = rotate(where, [*laps[3], far], bases, 5 * rows, 8 * rows, (early,), (act_mate,))
    parts = spread(terms, CHIPS)
    act_pair = jnp.concatenate([act_half, act_mate], axis=0)
    one = hop(act_pair, act_pair)
    two = hop(act_pair, act_pair, 2)
    own = spread(summed(parts, 8, 8, one + two), CHIPS)
    three = hop(*two)
    four = hop(two[0][:, : cols // 2], two[1][:, cols // 2 :], 2)
    (own,) = gate([own], three + four)
    other = swap(own, "c")

    acts = [x.reshape(2, 2, half, cols) for x in (act_pair, one[1], two[1], three[1], three[0], two[0], one[0])]
    acts += [x.reshape(2, 2, half, cols // 2) for x in four]
    return call(
        coeffs_kernel,
        jax.ShapeDtypeStruct((cols, width), jnp.float32),
        [where] + acts + [x.reshape(8, rows, width) for x in (own, other)],
        [SMEM] + [VMEM] * 11,
        flops=703 * 10**6,
        moved=5 * 10**6,
        out_specs=VMEM,
        scratch_shapes=[
            pltpu.VMEM((NZ, 2, 2, half, cols), jnp.bfloat16),
        ],
    )


def solution(mesh):
    fine = Mesh(mesh.devices.reshape(8, 2, 2, 4, 2), ("z", "xh", "xl", "y", "c"))
    return jax.shard_map(
        per_device,
        mesh=fine,
        in_specs=(P(NARROW, WIDE), P(WIDE, NARROW), P(WIDE, NARROW), P(NARROW, WIDE)),
        out_specs=P(NARROW, WIDE),
        check_vma=False,
    )
```

```python
import jax
import jax.numpy as jnp
from jax import lax
from jax.experimental import pallas as pl
from jax.experimental.pallas import tpu as pltpu
from jax.sharding import Mesh, PartitionSpec as P

SEQS = 4
NZ = 8
CHIPS, NARROW, WIDE = ("xl", "y"), ("xl", "y", "c"), ("z", "xh")


def shift(x, axis, by, size):
    return lax.ppermute(x, axis, [(i, (i + by) % size) for i in range(size)])


def swap(x, axis):
    return lax.ppermute(x, axis, [(0, 1), (1, 0)])


def dot(x, y):
    return jnp.dot(x, y, preferred_element_type=jnp.float32)


VMEM = pl.BlockSpec(memory_space=pltpu.VMEM)
ANY = pl.BlockSpec(memory_space=pl.ANY)
SMEM = pl.BlockSpec(memory_space=pltpu.SMEM)


def call(body, out, ins, specs, after=(), flops=10**6, moved=10**6, grant=16, **more):
    def kernel(*refs):
        body(*refs[: len(ins)], *refs[len(ins) + len(after) :])

    return pl.pallas_call(
        kernel,
        out_shape=out,
        in_specs=list(specs) + [ANY] * len(after),
        compiler_params=pltpu.CompilerParams(vmem_limit_bytes=grant * 1024 * 1024),
        cost_estimate=pl.CostEstimate(flops=flops, bytes_accessed=moved, transcendentals=0),
        **more,
    )(*ins, *after)


def gate(live, after=()):
    live = list(live)
    return call(
        lambda *refs: None,
        [jax.ShapeDtypeStruct(x.shape, x.dtype) for x in live],
        live,
        [VMEM] * len(live),
        after,
        out_specs=[VMEM] * len(live),
        input_output_aliases={k: k for k in range(len(live))},
    )


def hop(up, down, by=1):
    return shift(up, "z", by, NZ), shift(down, "z", -by, NZ)


def lap(x, only=None):
    steps = [(z, c, (z + 1 - 2 * c) % NZ) for z in range(NZ) for c in (0, 1) if only in (None, c)]
    return lax.ppermute(x, ("z", "c"), [(2 * z + c, 2 * to + c) for z, c, to in steps])


def join(*arrays, cols=None, after=()):
    cols = [cols or x.shape[1] for x in arrays]

    def body(*refs):
        start = 0
        for ref, col in zip(refs, cols):
            refs[-1][:, start : start + col] = ref[:, :col]
            start += col

    out = jax.ShapeDtypeStruct((arrays[0].shape[0], sum(cols)), arrays[0].dtype)
    return call(body, out, arrays, [VMEM] * len(arrays), after, out_specs=VMEM)


def rotate(where, blocks, bases, start, total, sums=(), after=(), fetch=True):
    parts = [block if isinstance(block, tuple) else (block,) for block in blocks]
    rows, depth, width = parts[0][0].shape[0], bases[0].shape[0], bases[0].shape[1]
    count, many = len(parts), sum(len(part) for part in parts)

    def body(where, *refs):
        refs, bases, (out, token, x, base, result, sems, out_sems, base_sems) = list(refs[:many]), refs[many : many + 2], refs[-8:]
        copies, slab = [], depth // 7
        for k in range(14 if fetch else 0):
            source = bases[k // 7].at[pl.ds(k % 7 * slab, slab)]
            copies.append(pltpu.make_async_copy(source, base.at[pl.ds(k * slab, slab)], base_sems.at[k]))
            copies[-1].start()
        for k, part in enumerate(parts):
            place, sem = x.at[pl.ds(k * rows, rows)], sems.at[k]
            copies.append(pltpu.make_async_copy(refs[0], place, sem))
            if len(part) == 1:
                copies[-1].start()
            else:
                for core in (0, 1):

                    @pl.when(where[1] == core)
                    def _():
                        pltpu.make_async_copy(refs[core], place, sem).start()

            refs = refs[len(part) :]
        for copy in copies:
            copy.wait()
        first, second = (base[:depth], base[depth:]) if fetch else (bases[0][...], bases[1][...])
        result[...] = (dot(x[:, :depth], first) + dot(x[:, depth:], second)).astype(result.dtype)
        token[...] = jnp.zeros_like(token)
        copies = []
        for k in range(count):
            here, there = pl.ds(k * rows, rows), pl.ds(start + k * rows, rows)
            copies.append(pltpu.make_async_copy(result.at[here], out.at[there], out_sems.at[k]))
            copies[-1].start()
        for copy in copies:
            copy.wait()

    out = [jax.ShapeDtypeStruct((total, width), jnp.bfloat16), jax.ShapeDtypeStruct((8, 128), jnp.float32)]
    scratch = [
        pltpu.VMEM((count * rows, 2 * depth), jnp.bfloat16),
        pltpu.VMEM((2 * depth if fetch else 16, width), jnp.bfloat16),
        pltpu.VMEM((count * rows, width), jnp.bfloat16),
        pltpu.SemaphoreType.DMA((count,)),
        pltpu.SemaphoreType.DMA((count,)),
        pltpu.SemaphoreType.DMA((14,)),
    ]
    ins = [where, *(x for part in parts for x in part), *bases, *sums]
    specs = [SMEM] + [ANY] * many + [ANY if fetch else VMEM] * 2 + [ANY] * len(sums)
    flops = 4 * count * rows * depth * width
    more = {"input_output_aliases": {len(ins) - 1: 0}} if sums else {}
    return call(body, out, ins, specs, after, flops, 5 * 10**6, 52, out_specs=[ANY, VMEM], scratch_shapes=scratch, **more)


def summed(parts, count, copies, after=()):
    rows, width = parts.shape[0] // count, parts.shape[1]

    def body(x, out):
        total = x[:rows].astype(jnp.float32)
        for k in range(1, count):
            total = total + x[k * rows : (k + 1) * rows].astype(jnp.float32)
        total = total.astype(out.dtype)
        for k in range(copies):
            out[k * rows : (k + 1) * rows] = total

    out = jax.ShapeDtypeStruct((copies * rows, width), jnp.bfloat16)
    return call(body, out, [parts], [VMEM], after, out_specs=VMEM)


def rotate_act(own, other, bases, after=()):
    rows = own.shape[0] // 8
    depth, width = bases[0].shape

    def body(mine, theirs, first, second, out):
        for k, ref in enumerate((mine, theirs)):
            total = dot(ref[:, :depth], first[...]) + dot(ref[:, depth:], second[...])
            for chip in range(8):
                out[chip, k] = total[chip * rows : (chip + 1) * rows].astype(out.dtype)

    out = jax.ShapeDtypeStruct((8, 2, rows, width), jnp.bfloat16)
    return call(body, out, [own, other, *bases], [VMEM] * 4, after, 2 * 10**8, 2 * 10**6, out_specs=VMEM)


def act_halves(where, mine, theirs, depth, after=()):
    half, width = mine.shape[0] // 2, mine.shape[1]

    def body(where, mine, theirs, out):
        start = pl.multiple_of(where[0] * half, half)
        for k in range(8):
            out[k * half : (k + 1) * half, :depth] = mine[pl.ds(start, half), width - depth :]
            out[k * half : (k + 1) * half, depth:] = theirs[pl.ds(start, half), width - depth :]

    out = jax.ShapeDtypeStruct((8 * half, 2 * depth), mine.dtype)
    return call(body, out, [where, mine, theirs], [SMEM, VMEM, VMEM], after, out_specs=VMEM)


def spread(x, axis):
    return lax.all_to_all(x, axis, 0, 0, tiled=True)


def coeffs_kernel(where, *refs):
    sources, (mine, other, out, act) = refs[:9], refs[9:]
    width = act.shape[-1] // 2
    for k, src in enumerate(sources[:7]):
        act[k + (k >= 4)] = src[...]
    for k, src in enumerate(sources[7:]):
        act[NZ // 2, :, :, :, k * width : (k + 1) * width] = src[...]
    xh, c, z = where[0], where[1], where[2]
    total = None
    for seq in range(SEQS):
        left, right = [], []
        for block in (2 * seq, 2 * seq + 1):
            rel = lax.rem(block - z + NZ, NZ)
            for side in (0, 1):
                halved = lax.rem(rel, NZ // 2) == 0
                up = rel > NZ // 2
                core = jnp.where(halved, side, jnp.where(up, 0, 1))
                place = jnp.where(up, 2 * (NZ - rel) - 1 + side, 2 * rel - 1 + side)
                place = jnp.where(halved, 7 * (rel // (NZ // 2)), place)
                parity = jnp.bitwise_xor(jnp.bitwise_xor(xh, side), c)
                left += [act[rel, xh, parity], act[rel, 1 - xh, parity]]
                right.append(jnp.where(core == c, mine[place], other[place]))
        coeffs = lax.dot_general(
            jnp.concatenate(left, axis=0),
            jnp.concatenate(right, axis=0),
            (((0,), (0,)), ((), ())),
            preferred_element_type=jnp.float32,
        )
        square = coeffs * coeffs
        total = square if total is None else total + square
    out[...] = total * (1.0 / SEQS)


def per_device(activations, grad_outputs, act_basis, grad_basis):
    z, xh, c = lax.axis_index("z"), lax.axis_index("xh"), lax.axis_index("c")
    where = jnp.stack([xh, c, z]).astype(jnp.int32)
    rows, half, width = grad_outputs.shape[0], grad_outputs.shape[0] // 2, grad_outputs.shape[1]
    cols = act_basis.shape[1]

    mate = swap(grad_outputs, "c")
    mine = join(grad_outputs, activations)
    theirs = swap(mine, "xh")
    act_basis2 = swap(act_basis, "xh")
    theirs_mate = swap(theirs, "c")
    act_copies = act_halves(where, mine, theirs, activations.shape[1])
    act_own = spread(act_copies, CHIPS)
    laps = [[join(grad_outputs, mate, after=(act_copies,)), join(theirs, theirs_mate, cols=width, after=(act_copies,))]]
    laps.append([lap(x) for x in laps[-1]])
    laps.append([lap(x) for x in laps[-1]])
    basis2 = swap(grad_basis, "c")
    (act_own,) = gate([act_own], (laps[1][0], act_basis2))
    act_oth = swap(act_own, "c")
    act_terms = rotate_act(act_own, act_oth, (act_basis, act_basis2))
    act_parts = spread(act_terms.reshape(8 * rows, cols), "z")
    laps[2] = [*gate(laps[2][:1], (act_terms,)), laps[2][1]]
    laps.append([lap(x) for x in laps[-1]])
    bases = grad_basis, basis2
    early, token = rotate(where, [tuple(laps[0]), *laps[1], *laps[2]], bases, 0, 8 * rows)
    laps[3] = [*gate(laps[3][:1], (token,)), laps[3][1]]
    far = tuple(lap(x, core) for core, x in enumerate(laps[3]))
    act_half = summed(act_parts, 8, 1, (token,))
    act_mate = swap(act_half, "xh")
    terms, _ = rotate(where, [*laps[3], far], bases, 5 * rows, 8 * rows, (early,), (act_mate,), False)
    parts = spread(terms, CHIPS)
    act_pair = jnp.concatenate([act_half, act_mate], axis=0)
    one = hop(act_pair, act_pair)
    two = hop(act_pair, act_pair, 2)
    own = spread(summed(parts, 8, 8, one + two), CHIPS)
    three = hop(*two)
    four = hop(two[0][:, : cols // 2], two[1][:, cols // 2 :], 2)
    (own,) = gate([own], three + four)
    other = swap(own, "c")

    acts = [x.reshape(2, 2, half, cols) for x in (act_pair, one[1], two[1], three[1], three[0], two[0], one[0])]
    acts += [x.reshape(2, 2, half, cols // 2) for x in four]
    return call(
        coeffs_kernel,
        jax.ShapeDtypeStruct((cols, width), jnp.float32),
        [where] + acts + [x.reshape(8, rows, width) for x in (own, other)],
        [SMEM] + [VMEM] * 11,
        flops=703 * 10**6,
        moved=5 * 10**6,
        out_specs=VMEM,
        scratch_shapes=[
            pltpu.VMEM((NZ, 2, 2, half, cols), jnp.bfloat16),
        ],
    )


def solution(mesh):
    fine = Mesh(mesh.devices.reshape(8, 2, 2, 4, 2), ("z", "xh", "xl", "y", "c"))
    return jax.shard_map(
        per_device,
        mesh=fine,
        in_specs=(P(NARROW, WIDE), P(WIDE, NARROW), P(WIDE, NARROW), P(NARROW, WIDE)),
        out_specs=P(NARROW, WIDE),
        check_vma=False,
    )
```
